128 devices in a mesh: row: 16 (over y, z), col: 8 (over x, core).
Axes of the slice: x: 4, y: 4, z: 4, core: 2. Of those that a mesh axis runs over, the one named last changes fastest.
Arguments:
- grads: bfloat16 [128, 640, 5760], P(('row', 'col')), may hold values from -24 to 24
- residuals: bfloat16 [128, 640, 5760], P(('row', 'col')), may hold values from -4 to 4
- q_prev: float32 [5760, 8], replicated, may hold values from -6 to 6
- vec_grads: float32 [25600, 1280], P(('row', 'col')), may hold values from -24 to 24
Outputs:
- new_residuals: bfloat16 [128, 640, 5760], P(('row', 'col'))
- decompressed: float32 [640, 5760], P(('row', 'col'))
- q_next: float32 [5760, 8], replicated
- vec_mean: float32 [200, 1280], replicated
The draws below stay inside these ranges and needn't reach their ends.
All inputs are finite; a program needn't handle non-finite values.
Results may differ from the reference program's by a relative error of at most 0.0077.
Values sent between devices are 32-bit elements; how exact they have to be, the bound alone decides.
No kernel may reach another device: no remote copies, remote signals or barrier semaphores. Data moves between devices by JAX's collectives and lax.ppermute only.
A program may use at most 64 MiB of HBM per device.

```python
import jax
import jax.numpy as jnp
from jax import lax

M_ROWS = 640
N_COLS = 5760
RANK = 8
CH = 1280
VEC = 200
REPLICAS = 128
N_ROW = 16
N_COL = 8


def strengthened(drawn, own_key, source, target, shards_of, factor):
    owner, partner = [(jnp.arange(drawn.shape[position]) // (drawn.shape[position] // shards_of)).reshape([-1 if axis == position else 1 for axis in range(drawn.ndim)]) for position in (source, target)]
    chosen = jax.random.permutation(own_key, shards_of)[partner]
    strong = (owner == chosen) | (owner == (partner + shards_of // 2) % shards_of)
    return jnp.where(strong, factor * drawn, drawn)


def block_levels(key, extent, pieces, low, largest):
    loudness = 1.0
    for dim, blocks in pieces:
        steps = jax.random.uniform(jax.random.fold_in(jax.random.fold_in(key, 6), dim), (blocks,), jnp.float32, low / len(pieces), largest / len(pieces))
        loudness = loudness * jnp.repeat(jnp.exp(steps), extent[dim] // blocks).reshape((-1,) + (1,) * (len(extent) - 1 - dim))
    return loudness


def scatter_about(stream_key, shape, deviation, reach, pieces=(), kind=jnp.bfloat16):
    drawn = jax.random.normal(stream_key, shape, jnp.float32) * deviation
    if len(pieces) > 0:
        drawn = block_levels(stream_key, shape, pieces, -0.22, 0.18) * drawn
    return jnp.clip(drawn, min=-reach, max=reach).astype(kind)


def heavy_noise(own_key, dims, width, bound, split, heavy, dtype=jnp.bfloat16):
    result = width * jax.random.normal(own_key, dims, jnp.float32)
    if split:
        result = result * block_levels(own_key, dims, split, -0.22, 0.18)
    return jnp.clip(strengthened(result, jax.random.fold_in(own_key, 3), *heavy), -bound, bound).astype(dtype)


def setup_inputs(seed: int = 0) -> dict:
    key_of = jax.random.split(jax.random.key(seed), 5)
    grads = heavy_noise(key_of[0], (REPLICAS, M_ROWS, N_COLS), 1.0, 24.0, ((0, 128),), (0, 1, 128, 5.5))
    residuals = scatter_about(key_of[1], (REPLICAS, M_ROWS, N_COLS), 0.5, 4.0, ((0, 128),))
    q_prev = scatter_about(key_of[2], (N_COLS, RANK), 1.0, 6.0, (), jnp.float32)
    vec_grads = scatter_about(key_of[3], (REPLICAS * VEC, CH), 4.0, 24.0, ((0, 128),), jnp.float32)
    return dict(grads=grads, residuals=residuals, q_prev=q_prev, vec_grads=vec_grads)


def reference(grads, residuals, q_prev, vec_grads):
    replicas = N_ROW * N_COL
    q_half = q_prev.astype(jnp.bfloat16)

    def p_term(carry, pair):
        wide = pair[0].astype(jnp.float32) + pair[1].astype(jnp.float32)
        compensated = wide.astype(jnp.bfloat16)
        return (carry + jnp.dot(compensated.astype(jnp.float32), q_half.astype(jnp.float32), preferred_element_type=jnp.float32), None)
    p_total, _ = lax.scan(p_term, jnp.zeros((M_ROWS, RANK), jnp.float32), (grads, residuals))
    gram = jnp.dot(p_total.T, p_total, precision=lax.Precision.HIGHEST)
    factor = jnp.linalg.cholesky(gram)
    p_orth = jax.scipy.linalg.solve_triangular(factor, p_total.T, lower=True).T
    p_half = p_orth.astype(jnp.bfloat16)

    def q_term(carry, pair):
        wide = pair[0].astype(jnp.float32) + pair[1].astype(jnp.float32)
        compensated = wide.astype(jnp.bfloat16)
        q_local = lax.dot_general(compensated.astype(jnp.float32), p_half.astype(jnp.float32), (((0,), (0,)), ((), ())), preferred_element_type=jnp.float32)
        fresh = wide - jnp.dot(p_orth, q_local.T, precision=lax.Precision.HIGHEST)
        return (carry + q_local, fresh.astype(jnp.bfloat16))
    q_total, new_residuals = lax.scan(q_term, jnp.zeros((N_COLS, RANK), jnp.float32), (grads, residuals))
    decompressed = jnp.dot(p_orth, q_total.T, precision=lax.Precision.HIGHEST) / replicas
    q_next = q_total / replicas
    vec_mean = jnp.sum(vec_grads.reshape(replicas, VEC, CH), axis=0) / replicas
    return (new_residuals, decompressed, q_next, vec_mean)
```

```python
import jax
import jax.numpy as jnp
from jax import lax
from jax.experimental import pallas as pl
from jax.experimental.pallas import tpu as pltpu
from jax.sharding import PartitionSpec as P

AXES = ("row", "col")
MIB = 1 << 20
LANES = 128
SUBS = 8
F32 = jnp.float32
BF16 = jnp.bfloat16
RING_BIT = {"x": 1, "z": 3, "y": 5}
AROUND = ("x", "y")
P_HOPS = (("x0", "x1", "y0", "z0", "z1", "y1"),) * 2
V_HOPS = (("y0", "z0", "x0", "x1", "z1", "y1"), ("z0", "x0", "y0", "y1", "x1", "z1"))
Q_HOPS = (("x0", "y0", "x1", "z0", "y1", "z1"), ("x1", "y1", "x0", "z1", "y0", "z0"))
HALVINGS = 2


def partner(index, hops):
    ring, level = hops[index & 1]
    bit = RING_BIT[ring]
    if level == "0":
        return index ^ (1 << bit)
    return index ^ ((3 if ring in AROUND else 2) << bit)


def swap(x, hops, step):
    pair = (hops[0][step], hops[1][step])
    return lax.ppermute(x, AXES, [(i, partner(i, pair)) for i in range(lax.axis_size(AXES))])


def swap_cores(x):
    return lax.ppermute(x, AXES, [(i, i ^ 1) for i in range(lax.axis_size(AXES))])


def place():
    return lax.axis_index("row") * lax.axis_size("col") + lax.axis_index("col")


def keeps_high(index, step):
    def of(hop):
        bit = RING_BIT[hop[0]]
        low, high = (index >> bit) & 1, (index >> (bit + 1)) & 1
        return low ^ high if hop[0] in AROUND else low

    core = index & 1
    return jnp.where(core == 0, of(V_HOPS[0][step]), of(V_HOPS[1][step])) == 1


def in_hbm(x):
    return pltpu.with_memory_space_constraint(x, pltpu.HBM)


def blocks(count):
    return jax.ShapeDtypeStruct((count, SUBS, LANES), F32)


def call(body, operands, outs, after=(), limit=12, **options):
    count = len(operands)

    def kernel(*refs):
        body(*refs[:count], *refs[count + len(after) :])

    return pl.pallas_call(
        kernel,
        in_specs=[pl.BlockSpec(memory_space=pltpu.VMEM)] * count + [pl.BlockSpec(memory_space=pl.ANY)] * len(after),
        out_specs=jax.tree.map(lambda _: pl.BlockSpec(memory_space=pltpu.VMEM), outs),
        out_shape=outs,
        compiler_params=pltpu.CompilerParams(vmem_limit_bytes=limit * MIB),
        **options,
    )(*operands, *after)


def left_product(grads, residuals, q_rows):
    _, rows, cols = grads.shape
    rank = q_rows.shape[0]
    parts = rows // LANES

    def body(g_hbm, r_hbm, q_hbm, p_ref, c_ref, g_ref, r_ref, q_ref, sems):
        copies = [pltpu.make_async_copy(q_hbm, q_ref, sems.at[2 * parts])]
        for i in range(parts):
            own = pl.ds(i * LANES, LANES)
            copies.append(pltpu.make_async_copy(g_hbm.at[0, own], g_ref.at[own], sems.at[2 * i]))
            copies.append(pltpu.make_async_copy(r_hbm.at[0, own], r_ref.at[own], sems.at[2 * i + 1]))
        for copy in copies:
            copy.start()
        copies[0].wait()
        q_half = q_ref[...].astype(BF16)
        for i in range(parts):
            own = slice(i * LANES, (i + 1) * LANES)
            copies[2 * i + 1].wait()
            copies[2 * i + 2].wait()
            compensated = (g_ref[own, :].astype(F32) + r_ref[own, :].astype(F32)).astype(BF16)
            c_ref[own, :] = compensated
            p_ref[i] = lax.dot_general(
                q_half, compensated, (((1,), (1,)), ((), ())), preferred_element_type=F32
            )

    whole = pltpu.VMEM((rows, cols), BF16)
    return pl.pallas_call(
        body,
        in_specs=[pl.BlockSpec(memory_space=pltpu.HBM)] * 3,
        out_specs=[pl.BlockSpec(memory_space=pltpu.VMEM)] * 4,
        out_shape=[blocks(parts), whole, whole, whole],
        scratch_shapes=[pltpu.VMEM((rank, cols), F32), pltpu.SemaphoreType.DMA((2 * parts + 1,))],
        compiler_params=pltpu.CompilerParams(vmem_limit_bytes=32 * MIB),
    )(in_hbm(grads), in_hbm(residuals), in_hbm(q_rows))


def right_product(p_tiles, p_other, compensated, after):
    tiles, rank, _ = p_tiles.shape
    rows, cols = compensated.shape
    out_tiles = cols // LANES
    count = (out_tiles + 1) // 2

    def body(p_ref, o_ref, c_ref, orth_ref, q_ref, keep_ref, send_ref):
        total = jnp.concatenate([p_ref[t] + o_ref[t] for t in range(tiles)], axis=1)
        gram = lax.dot_general(
            total, total, (((1,), (1,)), ((), ())), precision=lax.Precision.HIGHEST, preferred_element_type=F32
        )
        sub = lax.broadcasted_iota(jnp.int32, (rank, 1), 0)
        for j in range(rank):
            scale = lax.rsqrt(gram[j : j + 1, j : j + 1])
            column = jnp.where(sub > j, gram[:, j : j + 1] * scale, 0.0)
            gram_row, total_row = gram[j : j + 1, :] * scale, total[j : j + 1, :] * scale
            gram = jnp.where(sub == j, gram_row, gram - column * gram_row)
            total = jnp.where(sub == j, total_row, total - column * total_row)
        orth_ref[...] = total
        half = total.astype(BF16)
        step = 9 * LANES
        for s in range(0, cols, step):
            part = lax.dot_general(
                half, c_ref[:, s : s + step], (((1,), (0,)), ((), ())), preferred_element_type=F32
            )
            for t in range(step // LANES):
                q_ref[s // LANES + t] = part[:, t * LANES : (t + 1) * LANES]
        core = place() & 1

        @pl.when(core == 0)
        def _():
            keep_ref[...] = q_ref[:count]
            send_ref[...] = q_ref[out_tiles - count :]

        @pl.when(core == 1)
        def _():
            send_ref[...] = q_ref[:count]
            keep_ref[...] = q_ref[out_tiles - count :]

    outs = [jax.ShapeDtypeStruct((rank, rows), F32), blocks(out_tiles), blocks(count), blocks(count)]
    return call(body, [p_tiles, p_other, compensated], outs, after)


def thirds(x):
    a = x.astype(BF16)
    rest = x - a.astype(F32)
    b = rest.astype(BF16)
    return a, b, (rest - b.astype(F32)).astype(BF16)


def factors(orth, q_tiles, own_rows, after):
    rank, rows = orth.shape
    tiles = q_tiles.shape[0]

    def body(p_ref, q_ref, left_ref, right_ref, own_ref):
        a, b, c = thirds(p_ref[...])
        left_ref[...] = jnp.concatenate([a, a, b, a, b, c], axis=0)
        for t in range(tiles):
            a, b, c = thirds(q_ref[t])
            right_ref[:, t * LANES : (t + 1) * LANES] = jnp.concatenate([a, b, a, c, b, a], axis=0)
        column = lax.broadcasted_iota(jnp.int32, (SUBS, rows), 1)
        row = lax.broadcasted_iota(jnp.int32, (SUBS, rows), 0)
        chosen = jnp.where(column == place() * own_rows + row, 1.0, 0.0)
        own_ref[...] = lax.dot_general(
            chosen, p_ref[...], (((1,), (1,)), ((), ())), precision=lax.Precision.HIGHEST, preferred_element_type=F32
        )

    outs = [
        jax.ShapeDtypeStruct((6 * rank, rows), BF16),
        jax.ShapeDtypeStruct((6 * rank, tiles * LANES), BF16),
        jax.ShapeDtypeStruct((SUBS, rank), F32),
    ]
    return call(body, [orth, q_tiles], outs, after)


def residual_rows(piece, left, right, grads, residuals, before, after):
    rows, cols = grads.shape
    step = 9 * LANES
    parts = cols // step
    own = slice(piece * LANES, (piece + 1) * LANES)

    def body(l_ref, r_ref, g_ref, e_ref, *rest):
        out_hbm, done_ref, stage, sems = rest[-4:]
        copies = []
        for j in range(parts):
            here = slice(j * step, (j + 1) * step)
            wide = g_ref[own, here].astype(F32) + e_ref[own, here].astype(F32)
            away = lax.dot_general(
                l_ref[:, own], r_ref[:, here], (((0,), (0,)), ((), ())), preferred_element_type=F32
            )
            stage[:, here] = (wide - away).astype(BF16)
            copies.append(
                pltpu.make_async_copy(stage.at[:, here], out_hbm.at[0, own, here], sems.at[j])
            )
            copies[-1].start()
        done_ref[...] = jnp.zeros_like(done_ref)
        for copy in copies:
            copy.wait()

    operands = [left, right, grads, residuals]
    vmem, anywhere = pl.BlockSpec(memory_space=pltpu.VMEM), pl.BlockSpec(memory_space=pl.ANY)
    others = ([] if before is None else [before]) + list(after)
    return pl.pallas_call(
        body,
        in_specs=[vmem] * 4 + [anywhere] * len(others),
        out_specs=[pl.BlockSpec(memory_space=pltpu.HBM), vmem],
        out_shape=[jax.ShapeDtypeStruct((1, rows, cols), BF16), blocks(1)],
        scratch_shapes=[pltpu.VMEM((LANES, cols), BF16), pltpu.SemaphoreType.DMA((parts,))],
        input_output_aliases={} if before is None else {4: 0},
        compiler_params=pltpu.CompilerParams(vmem_limit_bytes=12 * MIB),
    )(*operands, *others)


def add(a, b, after=()):
    def body(a_ref, b_ref, out_ref):
        out_ref[...] = a_ref[...] + b_ref[...]

    return call(body, [a, b], blocks(a.shape[0]), after)


def split_vectors(vec, after):
    height, width = vec.shape
    across = width // LANES
    half = height // SUBS * across // 2

    def body(vec_ref, keep_ref, send_ref):
        def copy(low_ref, high_ref):
            for t in range(2 * half):
                y, x = t // across * SUBS, t % across * LANES
                tile = vec_ref[y : y + SUBS, x : x + LANES]
                if t < half:
                    low_ref[t] = tile
                else:
                    high_ref[t - half] = tile

        core = place() & 1

        @pl.when(core == 0)
        def _():
            copy(keep_ref, send_ref)

        @pl.when(core == 1)
        def _():
            copy(send_ref, keep_ref)

    return call(body, [vec], [blocks(half), blocks(half)], after)


def halve(step, a, b, after):
    size = a.shape[0]
    part = (size + 1) // 2

    def body(a_ref, b_ref, keep_ref, send_ref):
        low = a_ref[:part] + b_ref[:part]
        high = a_ref[size - part :] + b_ref[size - part :]
        flag = keeps_high(place(), step)
        keep_ref[...] = jnp.where(flag, high, low)
        send_ref[...] = jnp.where(flag, low, high)

    return call(body, [a, b], [blocks(part), blocks(part)], after)


def join(step, size, mine, other, after):
    part = mine.shape[0]

    def body(mine_ref, other_ref, out_ref):
        flag = keeps_high(place(), step)
        mine, other = mine_ref[...], other_ref[...]
        out_ref[size - part :] = jnp.where(flag, mine, other)
        out_ref[:part] = jnp.where(flag, other, mine)

    return call(body, [mine, other], blocks(size), after)


def join_vectors(mine, other, shape, replicas, after):
    height, width = shape
    across = width // LANES
    half = mine.shape[0]

    def body(mine_ref, other_ref, vec_ref):
        def copy(low_ref, high_ref):
            for t in range(2 * half):
                y, x = t // across * SUBS, t % across * LANES
                tile = low_ref[t] if t < half else high_ref[t - half]
                vec_ref[y : y + SUBS, x : x + LANES] = tile * (1.0 / replicas)

        core = place() & 1

        @pl.when(core == 0)
        def _():
            copy(mine_ref, other_ref)

        @pl.when(core == 1)
        def _():
            copy(other_ref, mine_ref)

    return call(body, [mine, other], jax.ShapeDtypeStruct(shape, F32), after)


def finish(mine, other, own, own_rows, tiles, replicas):
    count, rank, _ = mine.shape

    def body(mine_ref, other_ref, own_ref, q_ref, d_ref):
        def write(low_ref, high_ref):
            columns = [own_ref[:own_rows, k : k + 1] for k in range(rank)]
            for t in range(tiles):
                mean = (low_ref[t] if t < count else high_ref[t - tiles + count]) * (1.0 / replicas)
                q_ref[:, t * LANES : (t + 1) * LANES] = mean
                out = columns[0] * mean[0:1, :]
                for k in range(1, rank):
                    out = out + columns[k] * mean[k : k + 1, :]
                d_ref[:, t * LANES : (t + 1) * LANES] = out

        core = place() & 1

        @pl.when(core == 0)
        def _():
            write(mine_ref, other_ref)

        @pl.when(core == 1)
        def _():
            write(other_ref, mine_ref)

    outs = [
        jax.ShapeDtypeStruct((rank, tiles * LANES), F32),
        jax.ShapeDtypeStruct((own_rows, tiles * LANES), F32),
    ]
    return call(body, [mine, other, own], outs)


def on_device(grads, residuals, q_prev, vec_grads):
    devices = lax.axis_size(AXES)
    steps = len(P_HOPS[0])
    p_tiles, compensated, g_here, r_here = left_product(grads, residuals, q_prev.T)

    got = swap(p_tiles, P_HOPS, 0)
    v_keep, v_send = split_vectors(vec_grads, [p_tiles])
    half = v_keep.shape[0]
    v_got = swap_cores(v_send)
    p_tiles = add(p_tiles, got, [v_send])
    sizes = [half]
    v_step = 0

    def advance(after):
        nonlocal v_keep, v_send, v_got, v_step
        if v_step < HALVINGS:
            v_keep, v_send = halve(v_step, v_keep, v_got, after)
            sizes.append(v_keep.shape[0])
            v_got = swap(v_send, V_HOPS, v_step)
        elif v_step < steps:
            v_keep = v_send = add(v_keep, v_got, after)
            v_got = swap(v_send, V_HOPS, v_step)
        elif v_step < steps + HALVINGS:
            back = steps + HALVINGS - 1 - v_step
            if back == HALVINGS - 1:
                v_keep = add(v_keep, v_got, after)
            else:
                v_keep = join(back + 1, sizes[back + 1], v_keep, v_got, after)
            v_send = v_keep
            v_got = swap(v_send, V_HOPS, back)
        elif v_step == steps + HALVINGS:
            v_send = v_keep = join(0, half, v_keep, v_got, after)
            v_got = swap_cores(v_send)
        elif v_step == steps + HALVINGS + 1:
            v_send = v_keep = join_vectors(v_keep, v_got, vec_grads.shape, devices, after)
        v_step += 1

    for step in range(1, steps):
        got = swap(p_tiles, P_HOPS, step)
        advance([p_tiles])
        p_tiles = add(p_tiles, got, [v_send])

    orth, q_tiles, q_keep, q_send = right_product(p_tiles, swap_cores(p_tiles), compensated, [])
    got = swap_cores(q_send)
    left, right, own = factors(orth, q_tiles, orth.shape[1] // devices, [q_send])
    q_sum = add(q_keep, got, [own])
    fresh = None
    pieces = grads.shape[1] // LANES
    for step in range(steps):
        got = swap(q_sum, Q_HOPS, step)
        advance([q_sum])
        after = [v_send]
        piece = step - (steps - pieces)
        if piece >= 0:
            fresh, done = residual_rows(piece, left, right, g_here, r_here, fresh, [q_sum, v_send])
            after = [done]
        q_sum = add(q_sum, got, after)

    other = swap_cores(q_sum)
    q_next, decompressed = finish(q_sum, other, own, orth.shape[1] // devices, q_tiles.shape[0], devices)
    return (fresh, decompressed, q_next.T, v_keep)


def solution(mesh):
    return jax.shard_map(
        on_device,
        mesh=mesh,
        in_specs=(P(AXES, None, None), P(AXES, None, None), P(), P(AXES, None)),
        out_specs=(P(AXES, None, None), P(AXES, None), P(), P()),
        check_vma=False,
    )
```

```python
import jax
import jax.numpy as jnp
from jax import lax
from jax.experimental import pallas as pl
from jax.experimental.pallas import tpu as pltpu
from jax.sharding import PartitionSpec as P

AXES = ("row", "col")
MIB = 1 << 20
LANES = 128
SUBS = 8
F32 = jnp.float32
BF16 = jnp.bfloat16
RING_BIT = {"x": 1, "z": 3, "y": 5}
AROUND = ("x", "y", "z")
P_HOPS = (("x0", "x1", "y0", "y1", "z1", "z0"), ("y0", "y1", "z0", "z1", "x1", "x0"))
Q_HOPS = (("x1", "z1", "z0", "y0", "x0", "y1"), ("y1", "x1", "x0", "z0", "y0", "z1"))
HALVINGS = (0, 2)
SLABS = (1, 0, 3, 0, 0, 1)
LAST_PARTS = 3
SHORT = pl.CostEstimate(flops=0, bytes_accessed=0, transcendentals=0)
LONG = pl.CostEstimate(flops=10_000_000_000, bytes_accessed=0, transcendentals=0)


def partner(index, hops):
    ring, level = hops[index & 1]
    bit = RING_BIT[ring]
    if level == "0":
        return index ^ (1 << bit)
    return index ^ ((3 if ring in AROUND else 2) << bit)


def swap(x, hops, step):
    pair = (hops[0][step], hops[1][step])
    return lax.ppermute(x, AXES, [(i, partner(i, pair)) for i in range(lax.axis_size(AXES))])


def swap_cores(x):
    return lax.ppermute(x, AXES, [(i, i ^ 1) for i in range(lax.axis_size(AXES))])


def place():
    return lax.axis_index("row") * lax.axis_size("col") + lax.axis_index("col")


def keeps_high(index, halving):
    def of(hop):
        bit = RING_BIT[hop[0]]
        low, high = (index >> bit) & 1, (index >> (bit + 1)) & 1
        if hop[1] == "1":
            return high
        return low ^ high if hop[0] in AROUND else low

    core = index & 1
    step = HALVINGS[halving]
    return jnp.where(core == 0, of(P_HOPS[0][step]), of(P_HOPS[1][step])) == 1


def in_hbm(x):
    return pltpu.with_memory_space_constraint(x, pltpu.HBM)


def blocks(count):
    return jax.ShapeDtypeStruct((count, SUBS, LANES), F32)


def call(body, operands, outs, after=(), cost=SHORT, limit=12):
    count = len(operands)

    def kernel(*refs):
        body(*refs[:count], *refs[count + len(after) :])

    return pl.pallas_call(
        kernel,
        in_specs=[pl.BlockSpec(memory_space=pltpu.VMEM)] * count + [pl.BlockSpec(memory_space=pl.ANY)] * len(after),
        out_specs=jax.tree.map(lambda _: pl.BlockSpec(memory_space=pltpu.VMEM), outs),
        out_shape=outs,
        compiler_params=pltpu.CompilerParams(vmem_limit_bytes=limit * MIB),
        cost_estimate=cost,
    )(*operands, *after)


def left_product(grads, residuals, q_rows):
    _, rows, cols = grads.shape
    rank = q_rows.shape[0]
    parts = rows // LANES

    wide = cols // LAST_PARTS
    pieces = [(i, 0, cols) for i in range(parts - 1)]
    pieces += [(parts - 1, j * wide, wide) for j in range(LAST_PARTS)]

    def body(g_hbm, r_hbm, q_hbm, p_ref, c_ref, g_ref, r_ref, q_ref, sems):
        copies = [pltpu.make_async_copy(q_hbm, q_ref, sems.at[2 * len(pieces)])]
        for n, (i, first, width) in enumerate(pieces):
            own = (pl.ds(i * LANES, LANES), pl.ds(first, width))
            copies.append(pltpu.make_async_copy(g_hbm.at[(0, *own)], g_ref.at[own], sems.at[2 * n]))
            copies.append(pltpu.make_async_copy(r_hbm.at[(0, *own)], r_ref.at[own], sems.at[2 * n + 1]))
        for copy in copies:
            copy.start()
        copies[0].wait()
        for n, (i, first, width) in enumerate(pieces):
            own = (slice(i * LANES, (i + 1) * LANES), slice(first, first + width))
            copies[2 * n + 1].wait()
            copies[2 * n + 2].wait()
            compensated = (g_ref[own].astype(F32) + r_ref[own].astype(F32)).astype(BF16)
            c_ref[own] = compensated
            part = lax.dot_general(
                q_ref[:, own[1]].astype(BF16),
                compensated,
                (((1,), (1,)), ((), ())),
                preferred_element_type=F32,
            )
            p_ref[i] = part if first == 0 else p_ref[i] + part

    whole = pltpu.VMEM((rows, cols), BF16)
    return pl.pallas_call(
        body,
        in_specs=[pl.BlockSpec(memory_space=pltpu.HBM)] * 3,
        out_specs=[pl.BlockSpec(memory_space=pltpu.VMEM)] * 4,
        out_shape=[blocks(parts), whole, whole, whole],
        scratch_shapes=[pltpu.VMEM((rank, cols), F32), pltpu.SemaphoreType.DMA((2 * len(pieces) + 1,))],
        compiler_params=pltpu.CompilerParams(vmem_limit_bytes=32 * MIB),
    )(in_hbm(grads), in_hbm(residuals), in_hbm(q_rows))


def product_tiles(half, c_ref, first, out_ref):
    count = out_ref.shape[0]
    for t in range(0, count, 8):
        width = min(8, count - t) * LANES
        here = pl.ds(pl.multiple_of((first + t) * LANES, LANES), width)
        part = lax.dot_general(half, c_ref[:, here], (((1,), (0,)), ((), ())), preferred_element_type=F32)
        for k in range(width // LANES):
            out_ref[t + k] = part[:, k * LANES : (k + 1) * LANES]


def right_product(p_tiles, p_other, compensated):
    tiles, rank, _ = p_tiles.shape
    rows, cols = compensated.shape
    out_tiles = cols // LANES
    count = (out_tiles + 1) // 2

    def body(p_ref, o_ref, c_ref, orth_ref, send_ref):
        total = jnp.concatenate([p_ref[t] + o_ref[t] for t in range(tiles)], axis=1)
        gram = lax.dot_general(
            total, total, (((1,), (1,)), ((), ())), precision=lax.Precision.HIGHEST, preferred_element_type=F32
        )
        sub = lax.broadcasted_iota(jnp.int32, (rank, 1), 0)
        for j in range(rank):
            scale = lax.rsqrt(gram[j : j + 1, j : j + 1])
            column = jnp.where(sub > j, gram[:, j : j + 1] * scale, 0.0)
            gram_row, total_row = gram[j : j + 1, :] * scale, total[j : j + 1, :] * scale
            gram = jnp.where(sub == j, gram_row, gram - column * gram_row)
            total = jnp.where(sub == j, total_row, total - column * total_row)
        orth_ref[...] = total
        first = jnp.where(place() & 1 == 0, out_tiles - count, 0)
        product_tiles(total.astype(BF16), c_ref, first, send_ref)

    outs = [jax.ShapeDtypeStruct((rank, rows), F32), blocks(count)]
    return call(body, [p_tiles, p_other, compensated], outs)


def own_product(orth, compensated, after):
    out_tiles = compensated.shape[1] // LANES
    count = (out_tiles + 1) // 2

    def body(orth_ref, c_ref, keep_ref):
        first = jnp.where(place() & 1 == 0, 0, out_tiles - count)
        product_tiles(orth_ref[...].astype(BF16), c_ref, first, keep_ref)

    return call(body, [orth, compensated], blocks(count), after, LONG)


def thirds(x):
    a = x.astype(BF16)
    rest = x - a.astype(F32)
    b = rest.astype(BF16)
    return a, b, (rest - b.astype(F32)).astype(BF16)


def factors(orth, q_keep, q_send, own_rows, tiles):
    rank, rows = orth.shape
    count = q_keep.shape[0]

    def body(p_ref, keep_ref, send_ref, left_ref, right_ref, own_ref):
        a, b, c = thirds(p_ref[...])
        left_ref[...] = jnp.concatenate([a, a, b, a, b, c], axis=0)

        def write(low_ref, high_ref):
            for t in range(tiles):
                a, b, c = thirds(low_ref[t] if t < count else high_ref[t - tiles + count])
                right_ref[:, t * LANES : (t + 1) * LANES] = jnp.concatenate([a, b, a, c, b, a], axis=0)

        core = place() & 1

        @pl.when(core == 0)
        def _():
            write(keep_ref, send_ref)

        @pl.when(core == 1)
        def _():
            write(send_ref, keep_ref)

        column = lax.broadcasted_iota(jnp.int32, (SUBS, rows), 1)
        row = lax.broadcasted_iota(jnp.int32, (SUBS, rows), 0)
        chosen = jnp.where(column == place() * own_rows + row, 1.0, 0.0)
        own_ref[...] = lax.dot_general(
            chosen, p_ref[...], (((1,), (1,)), ((), ())), precision=lax.Precision.HIGHEST, preferred_element_type=F32
        )

    outs = [
        jax.ShapeDtypeStruct((6 * rank, rows), BF16),
        jax.ShapeDtypeStruct((6 * rank, tiles * LANES), BF16),
        jax.ShapeDtypeStruct((SUBS, rank), F32),
    ]
    return call(body, [orth, q_keep, q_send], outs, cost=LONG)


def residual_rows(first, count, left, right, grads, residuals, before, after):
    rows, cols = grads.shape
    step = 9 * LANES
    parts = cols // step
    own = slice(first * LANES, (first + count) * LANES)

    def body(l_ref, r_ref, g_ref, e_ref, *rest):
        out_hbm, done_ref, stage, sems = rest[-4:]
        copies = []
        for j in range(parts):
            here = slice(j * step, (j + 1) * step)
            wide = g_ref[own, here].astype(F32) + e_ref[own, here].astype(F32)
            away = lax.dot_general(
                l_ref[:, own], r_ref[:, here], (((0,), (0,)), ((), ())), preferred_element_type=F32
            )
            stage[:, here] = (wide - away).astype(BF16)
            copies.append(
                pltpu.make_async_copy(stage.at[:, here], out_hbm.at[0, own, here], sems.at[j])
            )
            copies[-1].start()
        done_ref[...] = jnp.zeros_like(done_ref)
        for copy in copies:
            copy.wait()

    operands = [left, right, grads, residuals]
    vmem, anywhere = pl.BlockSpec(memory_space=pltpu.VMEM), pl.BlockSpec(memory_space=pl.ANY)
    others = ([] if before is None else [before]) + list(after)
    return pl.pallas_call(
        body,
        in_specs=[vmem] * 4 + [anywhere] * len(others),
        out_specs=[pl.BlockSpec(memory_space=pltpu.HBM), vmem],
        out_shape=[jax.ShapeDtypeStruct((1, rows, cols), BF16), blocks(1)],
        scratch_shapes=[pltpu.VMEM((count * LANES, cols), BF16), pltpu.SemaphoreType.DMA((parts,))],
        input_output_aliases={} if before is None else {4: 0},
        compiler_params=pltpu.CompilerParams(vmem_limit_bytes=12 * MIB),
        cost_estimate=LONG,
    )(*operands, *others)


def add(a, b, after=(), cost=SHORT):
    def body(a_ref, b_ref, out_ref):
        out_ref[...] = a_ref[...] + b_ref[...]

    return call(body, [a, b], blocks(a.shape[0]), after, cost)


def hold(x, after):
    def body(x_ref, out_ref):
        out_ref[...] = x_ref[...]

    return call(body, [x], blocks(x.shape[0]), after, LONG)


def marker(after):
    def body(out_ref):
        out_ref[...] = jnp.zeros_like(out_ref)

    return call(body, [], blocks(1), after, LONG)


def first_half(vec, other, after):
    height, width = vec.shape
    across = width // LANES
    half = height // SUBS * across // 2
    part = (half + 1) // 2

    def body(vec_ref, other_ref, keep_ref, send_ref):
        def copy(first, out_ref):
            for t in range(part):
                y, x = (first + t) // across * SUBS, (first + t) % across * LANES
                here = (slice(y, y + SUBS), slice(x, x + LANES))
                out_ref[t] = vec_ref[here] + other_ref[here]

        index = place()
        high = keeps_high(index, 0)
        for core in (0, 1):
            for up in (False, True):
                low_ref, high_ref = (send_ref, keep_ref) if up else (keep_ref, send_ref)

                @pl.when((index & 1 == core) & (high if up else ~high))
                def _(core=core, low_ref=low_ref, high_ref=high_ref):
                    copy(core * half, low_ref)
                    copy(core * half + half - part, high_ref)

    return call(body, [vec, other], [blocks(part), blocks(part)], after, LONG)


def halve(halving, a, b, after):
    size = a.shape[0]
    part = (size + 1) // 2

    def body(a_ref, b_ref, keep_ref, send_ref):
        low = a_ref[:part] + b_ref[:part]
        high = a_ref[size - part :] + b_ref[size - part :]
        flag = keeps_high(place(), halving)
        keep_ref[...] = jnp.where(flag, high, low)
        send_ref[...] = jnp.where(flag, low, high)

    return call(body, [a, b], [blocks(part), blocks(part)], after, LONG)


def join(halving, size, mine, other, after):
    part = mine.shape[0]

    def body(mine_ref, other_ref, out_ref):
        flag = keeps_high(place(), halving)
        mine, other = mine_ref[...], other_ref[...]
        out_ref[size - part :] = jnp.where(flag, mine, other)
        out_ref[:part] = jnp.where(flag, other, mine)

    return call(body, [mine, other], blocks(size), after, LONG)


def join_vectors(mine, other, shape, replicas, after):
    across = shape[1] // LANES
    half = mine.shape[0]

    def body(mine_ref, other_ref, vec_ref, done_ref):
        done_ref[...] = jnp.zeros_like(done_ref)

        def write(low_ref, high_ref):
            for t in range(2 * half):
                y, x = t // across * SUBS, t % across * LANES
                tile = low_ref[t] if t < half else high_ref[t - half]
                vec_ref[y : y + SUBS, x : x + LANES] = tile * (1.0 / replicas)

        core = place() & 1

        @pl.when(core == 0)
        def _():
            write(mine_ref, other_ref)

        @pl.when(core == 1)
        def _():
            write(other_ref, mine_ref)

    return call(body, [mine, other], [jax.ShapeDtypeStruct(shape, F32), blocks(1)], after, LONG)


def finish(mine, other, own, own_rows, tiles, replicas, after):
    count, rank, _ = mine.shape

    def body(mine_ref, other_ref, own_ref, q_ref, d_ref):
        def write(low_ref, high_ref):
            columns = [own_ref[:own_rows, k : k + 1] for k in range(rank)]
            for t in range(tiles):
                mean = (low_ref[t] if t < count else high_ref[t - tiles + count]) * (1.0 / replicas)
                q_ref[:, t * LANES : (t + 1) * LANES] = mean
                out = columns[0] * mean[0:1, :]
                for k in range(1, rank):
                    out = out + columns[k] * mean[k : k + 1, :]
                d_ref[:, t * LANES : (t + 1) * LANES] = out

        core = place() & 1

        @pl.when(core == 0)
        def _():
            write(mine_ref, other_ref)

        @pl.when(core == 1)
        def _():
            write(other_ref, mine_ref)

    outs = [
        jax.ShapeDtypeStruct((rank, tiles * LANES), F32),
        jax.ShapeDtypeStruct((own_rows, tiles * LANES), F32),
    ]
    return call(body, [mine, other, own], outs, after)


def on_device(grads, residuals, q_prev, vec_grads):
    devices = lax.axis_size(AXES)
    steps = len(P_HOPS[0])
    tiles = grads.shape[2] // LANES
    own_rows = grads.shape[1] // devices
    half = vec_grads.size // (2 * SUBS * LANES)
    sizes = [half]
    for _ in HALVINGS:
        sizes.append((sizes[-1] + 1) // 2)
    v_other = swap_cores(vec_grads)
    p, compensated, g_here, r_here = left_product(grads, residuals, q_prev.T)

    v_keep = v_send = v_got = None
    for step in range(steps):
        got = swap(p, P_HOPS, step)
        after = []
        if step != 1:
            if step == 0:
                v_keep, v_send = first_half(vec_grads, v_other, [p])
            elif step in HALVINGS:
                v_keep, v_send = halve(HALVINGS.index(step), v_keep, v_got, [p])
            elif step < steps - 1:
                v_keep = v_send = add(v_keep, v_got, [p], LONG)
            else:
                v_keep = v_send = hold(v_keep, [p])
            if step != 4:
                v_got = swap(v_send, P_HOPS, step)
            after = [marker([v_send])]
        p = add(p, got, after)

    orth, q_send = right_product(p, swap_cores(p), compensated)
    got = swap_cores(q_send)
    q_keep = own_product(orth, compensated, [q_send])
    left, right, own = factors(orth, q_keep, q_send, own_rows, tiles)
    q = add(q_keep, got, [left])
    fresh = None
    for step in range(steps):
        got = swap(q, Q_HOPS, step)
        after = [q]
        if step == steps - 1:
            fresh, done = residual_rows(sum(SLABS[:step]), SLABS[step], left, right, g_here, r_here, fresh, after)
            after = [done]
        if step in (0, 1, 3):
            v_keep = add(v_keep, v_got, after, LONG)
        elif step > 3:
            v_keep = join(steps - 1 - step, sizes[steps - 1 - step], v_keep, v_got, after)
        if step != 2:
            v_got = swap(v_keep, Q_HOPS, step) if step < steps - 1 else swap_cores(v_keep)
        if SLABS[step] and step < steps - 1:
            fresh, done = residual_rows(
                sum(SLABS[:step]), SLABS[step], left, right, g_here, r_here, fresh, [q, v_keep]
            )
        else:
            done = marker([q, v_keep])
        q = add(q, got, [done])

    other = swap_cores(q)
    vec_mean, done = join_vectors(v_keep, v_got, vec_grads.shape, devices, [q])
    q_next, decompressed = finish(q, other, own, own_rows, tiles, devices, [done])
    return (fresh, decompressed, q_next.T, vec_mean)


def solution(mesh):
    return jax.shard_map(
        on_device,
        mesh=mesh,
        in_specs=(P(AXES, None, None), P(AXES, None, None), P(), P(AXES, None)),
        out_specs=(P(AXES, None, None), P(AXES, None), P(), P()),
        check_vma=False,
    )
```

```python
import jax
import jax.numpy as jnp
from jax import lax
from jax.experimental import pallas as pl
from jax.experimental.pallas import tpu as pltpu
from jax.sharding import PartitionSpec as P

AXES = ("row", "col")
MIB = 1 << 20
LANES = 128
SUBS = 8
F32 = jnp.float32
BF16 = jnp.bfloat16
RING_BIT = {"x": 1, "z": 3, "y": 5}
AROUND = ("x", "y", "z")
P_HOPS = (("x0", "x1", "y0", "y1", "z1", "z0"), ("y0", "y1", "z0", "z1", "x1", "x0"))
Q_HOPS = (("x1", "z1", "y0", "z0", "x0", "y1"), ("y1", "x1", "z0", "x0", "y0", "z1"))
HALVINGS = (0, 2)
SLABS = (1, 0, 0, 3, 0, 1)
LAST_PARTS = 3
SHORT = pl.CostEstimate(flops=0, bytes_accessed=0, transcendentals=0)
LONG = pl.CostEstimate(flops=10_000_000_000, bytes_accessed=0, transcendentals=0)


def partner(index, hops):
    ring, level = hops[index & 1]
    bit = RING_BIT[ring]
    if level == "0":
        return index ^ (1 << bit)
    return index ^ ((3 if ring in AROUND else 2) << bit)


def swap(x, hops, step):
    pair = (hops[0][step], hops[1][step])
    return lax.ppermute(x, AXES, [(i, partner(i, pair)) for i in range(lax.axis_size(AXES))])


def swap_cores(x):
    return lax.ppermute(x, AXES, [(i, i ^ 1) for i in range(lax.axis_size(AXES))])


def place():
    return lax.axis_index("row") * lax.axis_size("col") + lax.axis_index("col")


def keeps_high(index, halving):
    def of(hop):
        bit = RING_BIT[hop[0]]
        low, high = (index >> bit) & 1, (index >> (bit + 1)) & 1
        if hop[1] == "1":
            return high
        return low ^ high if hop[0] in AROUND else low

    core = index & 1
    step = HALVINGS[halving]
    return jnp.where(core == 0, of(P_HOPS[0][step]), of(P_HOPS[1][step])) == 1


def in_hbm(x):
    return pltpu.with_memory_space_constraint(x, pltpu.HBM)


def blocks(count):
    return jax.ShapeDtypeStruct((count, SUBS, LANES), F32)


def call(body, operands, outs, after=(), cost=SHORT, limit=12):
    count = len(operands)

    def kernel(*refs):
        body(*refs[:count], *refs[count + len(after) :])

    return pl.pallas_call(
        kernel,
        in_specs=[pl.BlockSpec(memory_space=pltpu.VMEM)] * count + [pl.BlockSpec(memory_space=pl.ANY)] * len(after),
        out_specs=jax.tree.map(lambda _: pl.BlockSpec(memory_space=pltpu.VMEM), outs),
        out_shape=outs,
        compiler_params=pltpu.CompilerParams(vmem_limit_bytes=limit * MIB),
        cost_estimate=cost,
    )(*operands, *after)


def left_product(grads, residuals, q_rows):
    _, rows, cols = grads.shape
    rank = q_rows.shape[0]
    parts = rows // LANES

    wide = cols // LAST_PARTS
    pieces = [(i, 0, cols) for i in range(parts - 1)]
    pieces += [(parts - 1, j * wide, wide) for j in range(LAST_PARTS)]

    def body(g_hbm, r_hbm, q_hbm, p_ref, c_ref, g_ref, r_ref, q_ref, sems):
        copies = [pltpu.make_async_copy(q_hbm, q_ref, sems.at[2 * len(pieces)])]
        for n, (i, first, width) in enumerate(pieces):
            own = (pl.ds(i * LANES, LANES), pl.ds(first, width))
            copies.append(pltpu.make_async_copy(g_hbm.at[(0, *own)], g_ref.at[own], sems.at[2 * n]))
            copies.append(pltpu.make_async_copy(r_hbm.at[(0, *own)], r_ref.at[own], sems.at[2 * n + 1]))
        for copy in copies:
            copy.start()
        copies[0].wait()
        for n, (i, first, width) in enumerate(pieces):
            own = (slice(i * LANES, (i + 1) * LANES), slice(first, first + width))
            copies[2 * n + 1].wait()
            copies[2 * n + 2].wait()
            compensated = (g_ref[own].astype(F32) + r_ref[own].astype(F32)).astype(BF16)
            c_ref[own] = compensated
            part = lax.dot_general(
                q_ref[:, own[1]].astype(BF16),
                compensated,
                (((1,), (1,)), ((), ())),
                preferred_element_type=F32,
            )
            p_ref[i] = part if first == 0 else p_ref[i] + part

    whole = pltpu.VMEM((rows, cols), BF16)
    return pl.pallas_call(
        body,
        in_specs=[pl.BlockSpec(memory_space=pltpu.HBM)] * 3,
        out_specs=[pl.BlockSpec(memory_space=pltpu.VMEM)] * 4,
        out_shape=[blocks(parts), whole, whole, whole],
        scratch_shapes=[pltpu.VMEM((rank, cols), F32), pltpu.SemaphoreType.DMA((2 * len(pieces) + 1,))],
        compiler_params=pltpu.CompilerParams(vmem_limit_bytes=32 * MIB),
    )(in_hbm(grads), in_hbm(residuals), in_hbm(q_rows))


def product_tiles(half, c_ref, first, out_ref):
    count = out_ref.shape[0]
    for t in range(0, count, 8):
        width = min(8, count - t) * LANES
        here = pl.ds(pl.multiple_of((first + t) * LANES, LANES), width)
        part = lax.dot_general(half, c_ref[:, here], (((1,), (0,)), ((), ())), preferred_element_type=F32)
        for k in range(width // LANES):
            out_ref[t + k] = part[:, k * LANES : (k + 1) * LANES]


def right_product(p_tiles, p_other, compensated):
    tiles, rank, _ = p_tiles.shape
    rows, cols = compensated.shape
    out_tiles = cols // LANES
    count = (out_tiles + 1) // 2

    def body(p_ref, o_ref, c_ref, orth_ref, send_ref):
        total = jnp.concatenate([p_ref[t] + o_ref[t] for t in range(tiles)], axis=1)
        gram = lax.dot_general(
            total, total, (((1,), (1,)), ((), ())), precision=lax.Precision.HIGHEST, preferred_element_type=F32
        )
        sub = lax.broadcasted_iota(jnp.int32, (rank, 1), 0)
        for j in range(rank):
            scale = lax.rsqrt(gram[j : j + 1, j : j + 1])
            column = jnp.where(sub > j, gram[:, j : j + 1] * scale, 0.0)
            gram_row, total_row = gram[j : j + 1, :] * scale, total[j : j + 1, :] * scale
            gram = jnp.where(sub == j, gram_row, gram - column * gram_row)
            total = jnp.where(sub == j, total_row, total - column * total_row)
        orth_ref[...] = total
        first = jnp.where(place() & 1 == 0, out_tiles - count, 0)
        product_tiles(total.astype(BF16), c_ref, first, send_ref)

    outs = [jax.ShapeDtypeStruct((rank, rows), F32), blocks(count)]
    return call(body, [p_tiles, p_other, compensated], outs)


def own_product(orth, compensated, after):
    out_tiles = compensated.shape[1] // LANES
    count = (out_tiles + 1) // 2

    def body(orth_ref, c_ref, keep_ref):
        first = jnp.where(place() & 1 == 0, 0, out_tiles - count)
        product_tiles(orth_ref[...].astype(BF16), c_ref, first, keep_ref)

    return call(body, [orth, compensated], blocks(count), after, LONG)


def thirds(x):
    a = x.astype(BF16)
    rest = x - a.astype(F32)
    b = rest.astype(BF16)
    return a, b, (rest - b.astype(F32)).astype(BF16)


def factors(orth, q_keep, q_send, own_rows, tiles):
    rank, rows = orth.shape
    count = q_keep.shape[0]

    def body(p_ref, keep_ref, send_ref, left_ref, right_ref, own_ref):
        a, b, c = thirds(p_ref[...])
        left_ref[...] = jnp.concatenate([a, a, b, a, b, c], axis=0)

        def write(low_ref, high_ref):
            for t in range(tiles):
                a, b, c = thirds(low_ref[t] if t < count else high_ref[t - tiles + count])
                right_ref[:, t * LANES : (t + 1) * LANES] = jnp.concatenate([a, b, a, c, b, a], axis=0)

        core = place() & 1

        @pl.when(core == 0)
        def _():
            write(keep_ref, send_ref)

        @pl.when(core == 1)
        def _():
            write(send_ref, keep_ref)

        column = lax.broadcasted_iota(jnp.int32, (SUBS, rows), 1)
        row = lax.broadcasted_iota(jnp.int32, (SUBS, rows), 0)
        chosen = jnp.where(column == place() * own_rows + row, 1.0, 0.0)
        own_ref[...] = lax.dot_general(
            chosen, p_ref[...], (((1,), (1,)), ((), ())), precision=lax.Precision.HIGHEST, preferred_element_type=F32
        )

    outs = [
        jax.ShapeDtypeStruct((6 * rank, rows), BF16),
        jax.ShapeDtypeStruct((6 * rank, tiles * LANES), BF16),
        jax.ShapeDtypeStruct((SUBS, rank), F32),
    ]
    return call(body, [orth, q_keep, q_send], outs, cost=LONG)


def residual_rows(first, count, left, right, grads, residuals, before, after):
    rows, cols = grads.shape
    step = 9 * LANES
    parts = cols // step
    own = slice(first * LANES, (first + count) * LANES)

    def body(l_ref, r_ref, g_ref, e_ref, *rest):
        out_hbm, done_ref, stage, sems = rest[-4:]
        copies = []
        for j in range(parts):
            here = slice(j * step, (j + 1) * step)
            wide = g_ref[own, here].astype(F32) + e_ref[own, here].astype(F32)
            away = lax.dot_general(
                l_ref[:, own], r_ref[:, here], (((0,), (0,)), ((), ())), preferred_element_type=F32
            )
            stage[:, here] = (wide - away).astype(BF16)
            copies.append(
                pltpu.make_async_copy(stage.at[:, here], out_hbm.at[0, own, here], sems.at[j])
            )
            copies[-1].start()
        done_ref[...] = jnp.zeros_like(done_ref)
        for copy in copies:
            copy.wait()

    operands = [left, right, grads, residuals]
    vmem, anywhere = pl.BlockSpec(memory_space=pltpu.VMEM), pl.BlockSpec(memory_space=pl.ANY)
    others = ([] if before is None else [before]) + list(after)
    return pl.pallas_call(
        body,
        in_specs=[vmem] * 4 + [anywhere] * len(others),
        out_specs=[pl.BlockSpec(memory_space=pltpu.HBM), vmem],
        out_shape=[jax.ShapeDtypeStruct((1, rows, cols), BF16), blocks(1)],
        scratch_shapes=[pltpu.VMEM((count * LANES, cols), BF16), pltpu.SemaphoreType.DMA((parts,))],
        input_output_aliases={} if before is None else {4: 0},
        compiler_params=pltpu.CompilerParams(vmem_limit_bytes=12 * MIB),
        cost_estimate=LONG,
    )(*operands, *others)


def add(a, b, after=(), cost=SHORT):
    def body(a_ref, b_ref, out_ref):
        out_ref[...] = a_ref[...] + b_ref[...]

    return call(body, [a, b], blocks(a.shape[0]), after, cost)


def hold(x, after):
    def body(x_ref, out_ref):
        out_ref[...] = x_ref[...]

    return call(body, [x], blocks(x.shape[0]), after, LONG)


def marker(after):
    def body(out_ref):
        out_ref[...] = jnp.zeros_like(out_ref)

    return call(body, [], blocks(1), after, LONG)


def first_half(vec, other, after):
    height, width = vec.shape
    across = width // LANES
    half = height // SUBS * across // 2
    part = (half + 1) // 2

    def body(vec_ref, other_ref, keep_ref, send_ref):
        def copy(first, out_ref):
            for t in range(part):
                y, x = (first + t) // across * SUBS, (first + t) % across * LANES
                here = (slice(y, y + SUBS), slice(x, x + LANES))
                out_ref[t] = vec_ref[here] + other_ref[here]

        index = place()
        high = keeps_high(index, 0)
        for core in (0, 1):
            for up in (False, True):
                low_ref, high_ref = (send_ref, keep_ref) if up else (keep_ref, send_ref)

                @pl.when((index & 1 == core) & (high if up else ~high))
                def _(core=core, low_ref=low_ref, high_ref=high_ref):
                    copy(core * half, low_ref)
                    copy(core * half + half - part, high_ref)

    return call(body, [vec, other], [blocks(part), blocks(part)], after, LONG)


def halve(halving, a, b, after):
    size = a.shape[0]
    part = (size + 1) // 2

    def body(a_ref, b_ref, keep_ref, send_ref):
        low = a_ref[:part] + b_ref[:part]
        high = a_ref[size - part :] + b_ref[size - part :]
        flag = keeps_high(place(), halving)
        keep_ref[...] = jnp.where(flag, high, low)
        send_ref[...] = jnp.where(flag, low, high)

    return call(body, [a, b], [blocks(part), blocks(part)], after, LONG)


def join(halving, size, mine, other, after):
    part = mine.shape[0]

    def body(mine_ref, other_ref, out_ref):
        flag = keeps_high(place(), halving)
        mine, other = mine_ref[...], other_ref[...]
        out_ref[size - part :] = jnp.where(flag, mine, other)
        out_ref[:part] = jnp.where(flag, other, mine)

    return call(body, [mine, other], blocks(size), after, LONG)


def join_vectors(mine, other, shape, replicas, after):
    across = shape[1] // LANES
    half = mine.shape[0]

    def body(mine_ref, other_ref, vec_ref, done_ref):
        done_ref[...] = jnp.zeros_like(done_ref)

        def write(low_ref, high_ref):
            for t in range(2 * half):
                y, x = t // across * SUBS, t % across * LANES
                tile = low_ref[t] if t < half else high_ref[t - half]
                vec_ref[y : y + SUBS, x : x + LANES] = tile * (1.0 / replicas)

        core = place() & 1

        @pl.when(core == 0)
        def _():
            write(mine_ref, other_ref)

        @pl.when(core == 1)
        def _():
            write(other_ref, mine_ref)

    return call(body, [mine, other], [jax.ShapeDtypeStruct(shape, F32), blocks(1)], after, LONG)


def finish(mine, other, own, own_rows, tiles, replicas, after):
    count, rank, _ = mine.shape

    def body(mine_ref, other_ref, own_ref, q_ref, d_ref):
        def write(low_ref, high_ref):
            columns = [own_ref[:own_rows, k : k + 1] for k in range(rank)]
            for t in range(tiles):
                mean = (low_ref[t] if t < count else high_ref[t - tiles + count]) * (1.0 / replicas)
                q_ref[:, t * LANES : (t + 1) * LANES] = mean
                out = columns[0] * mean[0:1, :]
                for k in range(1, rank):
                    out = out + columns[k] * mean[k : k + 1, :]
                d_ref[:, t * LANES : (t + 1) * LANES] = out

        core = place() & 1

        @pl.when(core == 0)
        def _():
            write(mine_ref, other_ref)

        @pl.when(core == 1)
        def _():
            write(other_ref, mine_ref)

    outs = [
        jax.ShapeDtypeStruct((rank, tiles * LANES), F32),
        jax.ShapeDtypeStruct((own_rows, tiles * LANES), F32),
    ]
    return call(body, [mine, other, own], outs, after)


def on_device(grads, residuals, q_prev, vec_grads):
    devices = lax.axis_size(AXES)
    steps = len(P_HOPS[0])
    tiles = grads.shape[2] // LANES
    own_rows = grads.shape[1] // devices
    half = vec_grads.size // (2 * SUBS * LANES)
    sizes = [half]
    for _ in HALVINGS:
        sizes.append((sizes[-1] + 1) // 2)
    v_other = swap_cores(vec_grads)
    p, compensated, g_here, r_here = left_product(grads, residuals, q_prev.T)

    v_keep = v_send = v_got = None
    for step in range(steps):
        got = swap(p, P_HOPS, step)
        after = []
        if step != 1:
            if step == 0:
                v_keep, v_send = first_half(vec_grads, v_other, [p])
            elif step in HALVINGS:
                v_keep, v_send = halve(HALVINGS.index(step), v_keep, v_got, [p])
            elif step < steps - 1:
                v_keep = v_send = add(v_keep, v_got, [p], LONG)
            else:
                v_keep = v_send = hold(v_keep, [p])
            if step != 4:
                v_got = swap(v_send, P_HOPS, step)
            after = [marker([v_send])]
        p = add(p, got, after)

    orth, q_send = right_product(p, swap_cores(p), compensated)
    got = swap_cores(q_send)
    q_keep = own_product(orth, compensated, [q_send])
    left, right, own = factors(orth, q_keep, q_send, own_rows, tiles)
    q = add(q_keep, got, [left])
    fresh = None
    for step in range(steps):
        got = swap(q, Q_HOPS, step)
        after = [q]
        if step == steps - 1:
            fresh, done = residual_rows(sum(SLABS[:step]), SLABS[step], left, right, g_here, r_here, fresh, after)
            after = [done]
        if step < 3:
            v_keep = add(v_keep, v_got, after, LONG)
        elif step > 3:
            v_keep = join(steps - 1 - step, sizes[steps - 1 - step], v_keep, v_got, after)
        if step != 3:
            v_got = swap(v_keep, Q_HOPS, step) if step < steps - 1 else swap_cores(v_keep)
        if SLABS[step] and step < steps - 1:
            fresh, done = residual_rows(
                sum(SLABS[:step]), SLABS[step], left, right, g_here, r_here, fresh, [q, v_keep]
            )
        else:
            done = marker([q, v_keep])
        q = add(q, got, [done])

    other = swap_cores(q)
    vec_mean, done = join_vectors(v_keep, v_got, vec_grads.shape, devices, [q])
    q_next, decompressed = finish(q, other, own, own_rows, tiles, devices, [done])
    return (fresh, decompressed, q_next.T, vec_mean)


def solution(mesh):
    return jax.shard_map(
        on_device,
        mesh=mesh,
        in_specs=(P(AXES, None, None), P(AXES, None, None), P(), P(AXES, None)),
        out_specs=(P(AXES, None, None), P(AXES, None), P(), P()),
        check_vma=False,
    )
```

```python
import jax
import jax.numpy as jnp
from jax import lax
from jax.experimental import pallas as pl
from jax.experimental.pallas import tpu as pltpu
from jax.sharding import PartitionSpec as P

AXES = ("row", "col")
MIB = 1 << 20
LANES = 128
SUBS = 8
F32 = jnp.float32
BF16 = jnp.bfloat16
RING_BIT = {"x": 1, "z": 3, "y": 5}
AROUND = ("x", "y", "z")
P_HOPS = (("x0", "x1", "y0", "y1", "z2", "z0"), ("y0", "y1", "z0", "z1", "x1", "x0"))
Q_HOPS = (("x1", "z1", "y0", "z0", "x0", "y1"), ("y1", "x1", "z0", "x0", "y0", "z1"))
HALVINGS = (0, 2)
SLABS = (1, 0, 0, 3, 0, 1)
LAST_PARTS = 3
SHORT = pl.CostEstimate(flops=0, bytes_accessed=0, transcendentals=0)
LONG = pl.CostEstimate(flops=10_000_000_000, bytes_accessed=0, transcendentals=0)


def partner(index, hops):
    ring, level = hops[index & 1]
    bit = RING_BIT[ring]
    if level == "0":
        return index ^ (1 << bit)
    return index ^ ((3 if level == "1" and ring in AROUND else 2) << bit)


def swap(x, hops, step):
    pair = (hops[0][step], hops[1][step])
    return lax.ppermute(x, AXES, [(i, partner(i, pair)) for i in range(lax.axis_size(AXES))])


def swap_cores(x):
    return lax.ppermute(x, AXES, [(i, i ^ 1) for i in range(lax.axis_size(AXES))])


def place():
    return lax.axis_index("row") * lax.axis_size("col") + lax.axis_index("col")


def keeps_high(index, halving):
    def of(hop):
        bit = RING_BIT[hop[0]]
        low, high = (index >> bit) & 1, (index >> (bit + 1)) & 1
        if hop[1] == "1":
            return high
        return low ^ high if hop[0] in AROUND else low

    core = index & 1
    step = HALVINGS[halving]
    return jnp.where(core == 0, of(P_HOPS[0][step]), of(P_HOPS[1][step])) == 1


def in_hbm(x):
    return pltpu.with_memory_space_constraint(x, pltpu.HBM)


def blocks(count):
    return jax.ShapeDtypeStruct((count, SUBS, LANES), F32)


def call(body, operands, outs, after=(), cost=SHORT, limit=12):
    count = len(operands)

    def kernel(*refs):
        body(*refs[:count], *refs[count + len(after) :])

    return pl.pallas_call(
        kernel,
        in_specs=[pl.BlockSpec(memory_space=pltpu.VMEM)] * count + [pl.BlockSpec(memory_space=pl.ANY)] * len(after),
        out_specs=jax.tree.map(lambda _: pl.BlockSpec(memory_space=pltpu.VMEM), outs),
        out_shape=outs,
        compiler_params=pltpu.CompilerParams(vmem_limit_bytes=limit * MIB),
        cost_estimate=cost,
    )(*operands, *after)


def left_product(grads, residuals, q_rows):
    _, rows, cols = grads.shape
    rank = q_rows.shape[0]
    parts = rows // LANES

    wide = cols // LAST_PARTS
    pieces = [(i, 0, cols) for i in range(parts - 1)]
    pieces += [(parts - 1, j * wide, wide) for j in range(LAST_PARTS)]

    def body(g_hbm, r_hbm, q_hbm, p_ref, c_ref, g_ref, r_ref, q_ref, sems):
        copies = [pltpu.make_async_copy(q_hbm, q_ref, sems.at[2 * len(pieces)])]
        for n, (i, first, width) in enumerate(pieces):
            own = (pl.ds(i * LANES, LANES), pl.ds(first, width))
            copies.append(pltpu.make_async_copy(g_hbm.at[(0, *own)], g_ref.at[own], sems.at[2 * n]))
            copies.append(pltpu.make_async_copy(r_hbm.at[(0, *own)], r_ref.at[own], sems.at[2 * n + 1]))
        for copy in copies:
            copy.start()
        copies[0].wait()
        for n, (i, first, width) in enumerate(pieces):
            own = (slice(i * LANES, (i + 1) * LANES), slice(first, first + width))
            copies[2 * n + 1].wait()
            copies[2 * n + 2].wait()
            compensated = (g_ref[own].astype(F32) + r_ref[own].astype(F32)).astype(BF16)
            c_ref[own] = compensated
            part = lax.dot_general(
                q_ref[:, own[1]].astype(BF16),
                compensated,
                (((1,), (1,)), ((), ())),
                preferred_element_type=F32,
            )
            p_ref[i] = part if first == 0 else p_ref[i] + part

    whole = pltpu.VMEM((rows, cols), BF16)
    return pl.pallas_call(
        body,
        in_specs=[pl.BlockSpec(memory_space=pltpu.HBM)] * 3,
        out_specs=[pl.BlockSpec(memory_space=pltpu.VMEM)] * 4,
        out_shape=[blocks(parts), whole, whole, whole],
        scratch_shapes=[pltpu.VMEM((rank, cols), F32), pltpu.SemaphoreType.DMA((2 * len(pieces) + 1,))],
        compiler_params=pltpu.CompilerParams(vmem_limit_bytes=32 * MIB),
    )(in_hbm(grads), in_hbm(residuals), in_hbm(q_rows))


def product_tiles(half, c_ref, first, out_ref):
    count = out_ref.shape[0]
    for t in range(0, count, 8):
        width = min(8, count - t) * LANES
        here = pl.ds(pl.multiple_of((first + t) * LANES, LANES), width)
        part = lax.dot_general(half, c_ref[:, here], (((1,), (0,)), ((), ())), preferred_element_type=F32)
        for k in range(width // LANES):
            out_ref[t + k] = part[:, k * LANES : (k + 1) * LANES]


def right_product(p_tiles, p_other, compensated):
    tiles, rank, _ = p_tiles.shape
    rows, cols = compensated.shape
    out_tiles = cols // LANES
    count = (out_tiles + 1) // 2

    def body(p_ref, o_ref, c_ref, orth_ref, send_ref):
        total = jnp.concatenate([p_ref[t] + o_ref[t] for t in range(tiles)], axis=1)
        gram = lax.dot_general(
            total, total, (((1,), (1,)), ((), ())), precision=lax.Precision.HIGHEST, preferred_element_type=F32
        )
        sub = lax.broadcasted_iota(jnp.int32, (rank, 1), 0)
        for j in range(rank):
            below = jnp.broadcast_to(jnp.where(sub > j, gram[:, j : j + 1], 0.0), gram.shape)
            scale = lax.rsqrt(jnp.broadcast_to(gram[j : j + 1, j : j + 1], gram.shape))
            gram_row, total_row = gram[j : j + 1, :] * scale[:1, :], total[j : j + 1, :] * scale[:1, :1]
            column = below * scale
            gram = jnp.where(sub == j, gram_row, gram - column * gram_row)
            total = jnp.where(sub == j, total_row, total - column[:, :1] * total_row)
        orth_ref[...] = total
        first = jnp.where(place() & 1 == 0, out_tiles - count, 0)
        product_tiles(total.astype(BF16), c_ref, first, send_ref)

    outs = [jax.ShapeDtypeStruct((rank, rows), F32), blocks(count)]
    return call(body, [p_tiles, p_other, compensated], outs)


def own_product(orth, compensated, after):
    out_tiles = compensated.shape[1] // LANES
    count = (out_tiles + 1) // 2

    def body(orth_ref, c_ref, keep_ref):
        first = jnp.where(place() & 1 == 0, 0, out_tiles - count)
        product_tiles(orth_ref[...].astype(BF16), c_ref, first, keep_ref)

    return call(body, [orth, compensated], blocks(count), after, LONG)


def thirds(x):
    a = x.astype(BF16)
    rest = x - a.astype(F32)
    b = rest.astype(BF16)
    return a, b, (rest - b.astype(F32)).astype(BF16)


def factors(orth, q_keep, q_send, own_rows, tiles):
    rank, rows = orth.shape
    count = q_keep.shape[0]

    def body(p_ref, keep_ref, send_ref, left_ref, right_ref, own_ref):
        a, b, c = thirds(p_ref[...])
        left_ref[...] = jnp.concatenate([a, a, b, a, b, c], axis=0)

        def write(low_ref, high_ref):
            for t in range(tiles):
                a, b, c = thirds(low_ref[t] if t < count else high_ref[t - tiles + count])
                right_ref[:, t * LANES : (t + 1) * LANES] = jnp.concatenate([a, b, a, c, b, a], axis=0)

        core = place() & 1

        @pl.when(core == 0)
        def _():
            write(keep_ref, send_ref)

        @pl.when(core == 1)
        def _():
            write(send_ref, keep_ref)

        column = lax.broadcasted_iota(jnp.int32, (SUBS, rows), 1)
        row = lax.broadcasted_iota(jnp.int32, (SUBS, rows), 0)
        chosen = jnp.where(column == place() * own_rows + row, 1.0, 0.0)
        own_ref[...] = lax.dot_general(
            chosen, p_ref[...], (((1,), (1,)), ((), ())), precision=lax.Precision.HIGHEST, preferred_element_type=F32
        )

    outs = [
        jax.ShapeDtypeStruct((6 * rank, rows), BF16),
        jax.ShapeDtypeStruct((6 * rank, tiles * LANES), BF16),
        jax.ShapeDtypeStruct((SUBS, rank), F32),
    ]
    return call(body, [orth, q_keep, q_send], outs, cost=LONG)


def residual_rows(first, count, left, right, grads, residuals, before, after):
    rows, cols = grads.shape
    step = 9 * LANES
    parts = cols // step
    own = slice(first * LANES, (first + count) * LANES)

    def body(l_ref, r_ref, g_ref, e_ref, *rest):
        out_hbm, done_ref, stage, sems = rest[-4:]
        copies = []
        for j in range(parts):
            here = slice(j * step, (j + 1) * step)
            wide = g_ref[own, here].astype(F32) + e_ref[own, here].astype(F32)
            away = lax.dot_general(
                l_ref[:, own], r_ref[:, here], (((0,), (0,)), ((), ())), preferred_element_type=F32
            )
            stage[:, here] = (wide - away).astype(BF16)
            copies.append(
                pltpu.make_async_copy(stage.at[:, here], out_hbm.at[0, own, here], sems.at[j])
            )
            copies[-1].start()
        done_ref[...] = jnp.zeros_like(done_ref)
        for copy in copies:
            copy.wait()

    operands = [left, right, grads, residuals]
    vmem, anywhere = pl.BlockSpec(memory_space=pltpu.VMEM), pl.BlockSpec(memory_space=pl.ANY)
    others = ([] if before is None else [before]) + list(after)
    return pl.pallas_call(
        body,
        in_specs=[vmem] * 4 + [anywhere] * len(others),
        out_specs=[pl.BlockSpec(memory_space=pltpu.HBM), vmem],
        out_shape=[jax.ShapeDtypeStruct((1, rows, cols), BF16), blocks(1)],
        scratch_shapes=[pltpu.VMEM((count * LANES, cols), BF16), pltpu.SemaphoreType.DMA((parts,))],
        input_output_aliases={} if before is None else {4: 0},
        compiler_params=pltpu.CompilerParams(vmem_limit_bytes=12 * MIB),
        cost_estimate=LONG,
    )(*operands, *others)


def add(a, b, after=(), cost=SHORT):
    def body(a_ref, b_ref, out_ref):
        out_ref[...] = a_ref[...] + b_ref[...]

    return call(body, [a, b], blocks(a.shape[0]), after, cost)


def hold(x, after):
    def body(x_ref, out_ref):
        out_ref[...] = x_ref[...]

    return call(body, [x], blocks(x.shape[0]), after, LONG)


def marker(after):
    def body(out_ref):
        out_ref[...] = jnp.zeros_like(out_ref)

    return call(body, [], blocks(1), after, LONG)


def first_half(vec, other, after):
    height, width = vec.shape
    across = width // LANES
    half = height // SUBS * across // 2
    part = (half + 1) // 2

    def body(vec_ref, other_ref, keep_ref, send_ref):
        def copy(first, out_ref):
            for t in range(part):
                y, x = (first + t) // across * SUBS, (first + t) % across * LANES
                here = (slice(y, y + SUBS), slice(x, x + LANES))
                out_ref[t] = vec_ref[here] + other_ref[here]

        index = place()
        high = keeps_high(index, 0)
        for core in (0, 1):
            for up in (False, True):
                low_ref, high_ref = (send_ref, keep_ref) if up else (keep_ref, send_ref)

                @pl.when((index & 1 == core) & (high if up else ~high))
                def _(core=core, low_ref=low_ref, high_ref=high_ref):
                    copy(core * half, low_ref)
                    copy(core * half + half - part, high_ref)

    return call(body, [vec, other], [blocks(part), blocks(part)], after, LONG)


def halve(halving, a, b, after):
    size = a.shape[0]
    part = (size + 1) // 2

    def body(a_ref, b_ref, keep_ref, send_ref):
        low = a_ref[:part] + b_ref[:part]
        high = a_ref[size - part :] + b_ref[size - part :]
        flag = keeps_high(place(), halving)
        keep_ref[...] = jnp.where(flag, high, low)
        send_ref[...] = jnp.where(flag, low, high)

    return call(body, [a, b], [blocks(part), blocks(part)], after, LONG)


def join(halving, size, mine, other, after):
    part = mine.shape[0]

    def body(mine_ref, other_ref, out_ref):
        flag = keeps_high(place(), halving)
        mine, other = mine_ref[...], other_ref[...]
        out_ref[size - part :] = jnp.where(flag, mine, other)
        out_ref[:part] = jnp.where(flag, other, mine)

    return call(body, [mine, other], blocks(size), after, LONG)


def join_vectors(mine, other, shape, replicas, after):
    across = shape[1] // LANES
    half = mine.shape[0]

    def body(mine_ref, other_ref, vec_ref, done_ref):
        done_ref[...] = jnp.zeros_like(done_ref)

        def write(low_ref, high_ref):
            for t in range(2 * half):
                y, x = t // across * SUBS, t % across * LANES
                tile = low_ref[t] if t < half else high_ref[t - half]
                vec_ref[y : y + SUBS, x : x + LANES] = tile * (1.0 / replicas)

        core = place() & 1

        @pl.when(core == 0)
        def _():
            write(mine_ref, other_ref)

        @pl.when(core == 1)
        def _():
            write(other_ref, mine_ref)

    return call(body, [mine, other], [jax.ShapeDtypeStruct(shape, F32), blocks(1)], after, LONG)


def finish(mine, other, own, own_rows, tiles, replicas, after):
    count, rank, _ = mine.shape

    def body(mine_ref, other_ref, own_ref, q_ref, d_ref):
        def write(low_ref, high_ref):
            columns = [own_ref[:own_rows, k : k + 1] for k in range(rank)]
            for t in range(tiles):
                mean = (low_ref[t] if t < count else high_ref[t - tiles + count]) * (1.0 / replicas)
                q_ref[:, t * LANES : (t + 1) * LANES] = mean
                out = columns[0] * mean[0:1, :]
                for k in range(1, rank):
                    out = out + columns[k] * mean[k : k + 1, :]
                d_ref[:, t * LANES : (t + 1) * LANES] = out

        core = place() & 1

        @pl.when(core == 0)
        def _():
            write(mine_ref, other_ref)

        @pl.when(core == 1)
        def _():
            write(other_ref, mine_ref)

    outs = [
        jax.ShapeDtypeStruct((rank, tiles * LANES), F32),
        jax.ShapeDtypeStruct((own_rows, tiles * LANES), F32),
    ]
    return call(body, [mine, other, own], outs, after)


def on_device(grads, residuals, q_prev, vec_grads):
    devices = lax.axis_size(AXES)
    steps = len(P_HOPS[0])
    tiles = grads.shape[2] // LANES
    own_rows = grads.shape[1] // devices
    half = vec_grads.size // (2 * SUBS * LANES)
    sizes = [half]
    for _ in HALVINGS:
        sizes.append((sizes[-1] + 1) // 2)
    v_other = swap_cores(vec_grads)
    p, compensated, g_here, r_here = left_product(grads, residuals, q_prev.T)

    v_keep = v_send = v_got = None
    for step in range(steps):
        got = swap(p, P_HOPS, step)
        after = []
        if step != 1:
            if step == 0:
                v_keep, v_send = first_half(vec_grads, v_other, [p])
            elif step in HALVINGS:
                v_keep, v_send = halve(HALVINGS.index(step), v_keep, v_got, [p])
            elif step < steps - 1:
                v_keep = v_send = add(v_keep, v_got, [p], LONG)
            else:
                v_keep = v_send = hold(v_keep, [p])
            if step != 4:
                v_got = swap(v_send, P_HOPS, step)
            after = [marker([v_send])]
        p = add(p, got, after)

    orth, q_send = right_product(p, swap_cores(p), compensated)
    got = swap_cores(q_send)
    q_keep = own_product(orth, compensated, [q_send])
    left, right, own = factors(orth, q_keep, q_send, own_rows, tiles)
    q = add(q_keep, got, [left])
    fresh = None
    for step in range(steps):
        got = swap(q, Q_HOPS, step)
        after = [q]
        if step == steps - 1:
            fresh, done = residual_rows(sum(SLABS[:step]), SLABS[step], left, right, g_here, r_here, fresh, after)
            after = [done]
        if step < 3:
            v_keep = add(v_keep, v_got, after, LONG)
        elif step > 3:
            v_keep = join(steps - 1 - step, sizes[steps - 1 - step], v_keep, v_got, after)
        if step != 3:
            v_got = swap(v_keep, Q_HOPS, step) if step < steps - 1 else swap_cores(v_keep)
        if SLABS[step] and step < steps - 1:
            fresh, done = residual_rows(
                sum(SLABS[:step]), SLABS[step], left, right, g_here, r_here, fresh, [q, v_keep]
            )
        else:
            done = marker([q, v_keep])
        q = add(q, got, [done])

    other = swap_cores(q)
    vec_mean, done = join_vectors(v_keep, v_got, vec_grads.shape, devices, [q])
    q_next, decompressed = finish(q, other, own, own_rows, tiles, devices, [done])
    return (fresh, decompressed, q_next.T, vec_mean)


def solution(mesh):
    return jax.shard_map(
        on_device,
        mesh=mesh,
        in_specs=(P(AXES, None, None), P(AXES, None, None), P(), P(AXES, None)),
        out_specs=(P(AXES, None, None), P(AXES, None), P(), P()),
        check_vma=False,
    )
```
